32 devices in a mesh: ctx: 16 (over z, y, core), head: 2 (over x).
Axes of the slice: x: 2, y: 2, z: 4, core: 2. Of those that a mesh axis runs over, the one named last changes fastest.
Arguments:
- mixer_input: bfloat16 [2, 4096, 8192], P(None, 'ctx', 'head'), may hold values from -6 to 6
- gate_input: bfloat16 [2, 4096, 8192], P(None, 'ctx', 'head'), may hold values from -6 to 6
- state_in: bfloat16 [2, 4096, 1024], P(None, 'ctx', 'head'), may hold values from -0.875 to 0.875
- state_out: bfloat16 [2, 4096, 1024], P(None, 'ctx', 'head'), may hold values from -0.875 to 0.875
- step_sizes: float32 [2, 4096, 128], P(None, 'ctx', 'head'), may hold values from 0.5 to 2
- decay_rates: float32 [128], P('head'), may hold values from 6.1035156e-05 to 0.05
- skip_gain: float32 [128], P('head'), may hold values from 0.5 to 2
- norm_gain: float32 [8192], P('head'), may hold values from 0.5 to 1.5
- out_weight: bfloat16 [8192, 4096], P('head', 'ctx'), may hold values from -0.0625 to 0.0625
- queries: bfloat16 [2, 4096, 4096], P(None, 'ctx', 'head'), may hold values from -4.375 to 4.375
- keys: bfloat16 [2, 4096, 1024], P(None, 'ctx', 'head'), may hold values from -4.375 to 4.375
- values: bfloat16 [2, 4096, 1024], P(None, 'ctx', 'head'), may hold values from -6 to 6
- doc_ids: int32 [2, 4096], P(None, 'ctx'), may hold values from 0 to 15, never falling along the last dimension, each value on 1 to 512 neighbouring positions
Outputs:
- mixer_out: bfloat16 [2, 4096, 4096], P(None, 'ctx', 'head')
- attn_out: bfloat16 [2, 4096, 4096], P(None, 'ctx', 'head')
The draws below stay inside these ranges and needn't reach their ends.
Inputs may be any that keep to these rules, and one draw needn't show every extreme that they name: `doc_ids`: along each sequence the ids never fall and every id occurs; each document has 1 to 512 positions, and one document of each sequence has exactly 512.
All inputs are finite; a program needn't handle non-finite values.
Results may differ from the reference program's by a relative error of at most 0.014.
Values may be sent and summed in bfloat16 or wider, within the bound.
A program may use at most 256 MiB of HBM per device.

```python
import math
import jax
import jax.numpy as jnp
import numpy as np
from jax import lax

D = 4096
H = 128
P_SIZE = 64
N = 128
G = 8
QH = 32
KH = 8
HD = 128
SPAN = 128
DOCS = 16
BATCH = 2
SEQ_DEV = 256
SEQ = 4096
INNER = 8192
HEAD_DEV = 64
REACH = 2


def draw_queries(key, part):
    drawn = jax.random.normal(jax.random.fold_in(key, 1), (BATCH, SEQ, QH, HD), jnp.float32)
    drawn = jnp.clip(drawn, -4.375, 4.375)
    return drawn.reshape(BATCH, SEQ, QH * HD).astype(jnp.bfloat16)


def draw_keys(key, part):
    drawn = jax.random.normal(jax.random.fold_in(key, 2), (BATCH, SEQ, KH, HD), jnp.float32)
    drawn = jnp.clip(drawn, -4.375, 4.375)
    return drawn.reshape(BATCH, SEQ, KH * HD).astype(jnp.bfloat16)


def shard_levels(own_key, shape, shards, least, high):
    factor_of, own = 1.0, jax.random.fold_in(own_key, 6)
    for position, blocks in shards:
        heights = jnp.exp(jax.random.uniform(jax.random.fold_in(own, position), (blocks,), jnp.float32, least / len(shards), high / len(shards)))
        factor_of = factor_of * jnp.repeat(heights, shape[position] // blocks).reshape([-1 if axis == position else 1 for axis in range(len(shape))])
    return factor_of


def split_up(count, total, limit, lean):
    portions = [(1 << 20) // math.isqrt(standing ** lean) + 1 for standing in range(2, count + 1)]
    rest, counts = total - limit - (count - 1), [1] * (count - 1)
    while rest > 0:
        free = [i for i in range(count - 1) if counts[i] < limit]
        whole, left = sum([portions[i] for i in free]), rest
        for i in free:
            extra = min(limit - counts[i], max(1, left * portions[i] // whole), rest)
            counts[i] = counts[i] + extra
            rest = rest - extra
    return np.array([limit] + counts)


def ragged(stream_key, number_of, total, most, lean):
    if number_of == 2:
        one = jax.random.randint(stream_key, (), max(1, total - most), min(most, total - 1) + 1)
        return jnp.stack([one, total - one])
    sizes = jnp.asarray(split_up(number_of, total, most, lean), jnp.int32)
    couples = (number_of - 1) // 2
    giver, receiver = sizes[1:1 + 2 * couples:2], sizes[2:2 + 2 * couples:2]
    room = jnp.minimum(giver - 1, most - receiver)
    moved = jax.random.randint(jax.random.fold_in(stream_key, 1), (couples,), 0, 1 << 20) % (room + 1)
    sizes = sizes.at[1:1 + 2 * couples:2].set(giver - moved).at[2:2 + 2 * couples:2].set(receiver + moved)
    return sizes[jax.random.permutation(jax.random.fold_in(stream_key, 2), number_of)]


def normal_values(key, extent, deviation, limit, shards=(), kind=jnp.bfloat16):
    values = jax.random.normal(key, extent, jnp.float32) * deviation
    if len(shards) > 0:
        values = shard_levels(key, extent, shards, -0.22, 0.18) * values
    return jnp.clip(values, min=-limit, max=limit).astype(kind)


def setup_inputs(seed: int = 0) -> dict:
    seeds = jax.random.split(jax.random.key(seed), 14)
    mixer_input = normal_values(seeds[0], (BATCH, SEQ, INNER), 1.0, 6.0, ((1, 16), (2, 2)))
    gate_input = normal_values(seeds[1], (BATCH, SEQ, INNER), 1.0, 6.0, ((1, 16), (2, 2)))
    state_in = normal_values(seeds[2], (BATCH, SEQ, G * N), 0.15, 0.875, ((1, 16), (2, 2)))
    state_out = normal_values(seeds[3], (BATCH, SEQ, G * N), 0.15, 0.875, ((1, 16), (2, 2)))
    step_sizes = jnp.clip(jnp.exp(math.log(2.0) - 1.3862944 * jax.random.uniform(seeds[4], (BATCH, SEQ, H), jnp.float32) ** shard_levels(seeds[4], (BATCH, SEQ, H), ((1, 16), (2, 2)), -0.2, 0.2)), 0.5, 2.0)
    decay_rates = jnp.clip(jnp.exp(math.log(0.05) - 6.7083283 * jax.random.uniform(seeds[5], (H,), jnp.float32) ** shard_levels(seeds[5], (H,), ((0, 2),), -0.2, 0.2)), 6.103515625e-05, 0.05)
    skip_gain = jnp.clip(0.5 + 1.5 * jax.random.uniform(seeds[6], (H,), jnp.float32) ** shard_levels(seeds[6], (H,), ((0, 2),), -0.2, 0.2), 0.5, 2.0)
    norm_gain = jnp.clip(1.0 + 0.1 * jax.random.normal(seeds[7], (INNER,), jnp.float32), 0.5, 1.5)
    out_weight = normal_values(seeds[8], (INNER, D), INNER ** -0.5, 0.0625, ((0, 2), (1, 16)))
    queries = draw_queries(jax.random.fold_in(seeds[13], 71), 0)
    keys = draw_keys(jax.random.fold_in(seeds[13], 71), 0)
    values = normal_values(seeds[11], (BATCH, SEQ, KH * HD), 1.0, 6.0, ((1, 16), (2, 2)))
    doc_ids = jax.vmap(lambda own: jnp.searchsorted(jnp.cumsum(ragged(own, DOCS, SEQ, SEQ // 8, 2)), jnp.arange(SEQ), side="right"))(jax.random.split(seeds[12], BATCH)).reshape((BATCH, SEQ)).astype(jnp.int32)
    return dict(mixer_input=mixer_input, gate_input=gate_input, state_in=state_in, state_out=state_out, step_sizes=step_sizes, decay_rates=decay_rates, skip_gain=skip_gain, norm_gain=norm_gain, out_weight=out_weight, queries=queries, keys=keys, values=values, doc_ids=doc_ids)


epsilon = 1e-05
lowest = -1e+30

def span_scan(inputs, widths, rates, writers, readers, documents, block, initial, initial_doc):
    batches, length, heads, channels = inputs.shape
    groups = writers.shape[2]
    repeat = heads // groups
    count = length // block

    def split(array):
        shaped = array.reshape((batches, count, block) + array.shape[2:])
        return jnp.moveaxis(shaped, 1, 0)
    order = jnp.arange(block, dtype=jnp.int32)
    causal = order[:, None] >= order[None, :]

    def advance(carry, pieces):
        state, state_doc = carry
        input_now, width_now, writer_now, reader_now, doc_now = pieces
        cumulative = jnp.cumsum(width_now * rates, axis=1)
        allowed = ((doc_now[:, :, None] == doc_now[:, None, :]) & causal)[..., None]
        spread = cumulative[:, :, None, :] - cumulative[:, None, :, :]
        decays = jnp.where(allowed, jnp.exp(-jnp.where(allowed, spread, 0.0)), 0.0)
        intersection = jnp.einsum('btgn,bsgn->btsg', reader_now, writer_now, preferred_element_type=jnp.float32)
        intersection = jnp.repeat(intersection, repeat, axis=3)
        mixing = (decays * intersection * width_now[:, None, :, :]).astype(jnp.bfloat16)
        within = jnp.einsum('btsh,bshp->bthp', mixing, input_now, preferred_element_type=jnp.float32)
        read_heads = jnp.repeat(reader_now, repeat, axis=2)
        living = (doc_now == state_doc[:, None]).astype(jnp.float32)
        carried = jnp.einsum('bthn,bhpn->bthp', read_heads, state.astype(jnp.bfloat16), preferred_element_type=jnp.float32)
        carried = carried * (jnp.exp(-cumulative) * living[:, :, None])[..., None]
        last_doc = doc_now[:, -1]
        ending = cumulative[:, -1:, :] - cumulative
        tailing = jnp.where((doc_now == last_doc[:, None])[..., None], jnp.exp(-ending), 0.0) * width_now
        write_heads = jnp.repeat(writer_now, repeat, axis=2)
        keeping = jnp.exp(-cumulative[:, -1, :]) * (last_doc == state_doc).astype(jnp.float32)[:, None]
        scaled = (tailing[..., None] * input_now.astype(jnp.float32)).astype(jnp.bfloat16)
        written = jnp.einsum('bshp,bshn->bhpn', scaled, write_heads, preferred_element_type=jnp.float32)
        state = state * keeping[:, :, None, None] + written
        return ((state, last_doc), within + carried)
    pieces = (split(inputs), split(widths), split(writers), split(readers), split(documents))
    (state, last_doc), outputs = lax.scan(advance, (initial, initial_doc), pieces)
    outputs = jnp.moveaxis(outputs, 0, 1).reshape(batches, length, heads, channels)
    return (outputs, state)

def gate_norm(gated, gain, groups):
    shaped = gated.reshape(gated.shape[:-1] + (groups, gated.shape[-1] // groups))
    factor = lax.rsqrt(lax.optimization_barrier(jnp.mean(shaped * shaped, axis=-1, keepdims=True)) + epsilon)
    return ((shaped * factor).reshape(gated.shape) * gain).astype(jnp.bfloat16)

def attention(queries, keys, values, doc_ids):
    repeat = QH // KH
    query_heads = queries.reshape(BATCH, SEQ, KH, repeat, HD)
    key_heads = keys.reshape(BATCH, SEQ, KH, HD)
    value_heads = values.reshape(BATCH, SEQ, KH, HD)
    window = (REACH + 1) * SEQ_DEV
    scale = HD ** (-0.5)

    def one_block(index):
        query_start = (index * SEQ_DEV).astype(jnp.int32)
        key_start = jnp.maximum(query_start - REACH * SEQ_DEV, 0).astype(jnp.int32)
        query_block = lax.dynamic_slice_in_dim(query_heads, query_start, SEQ_DEV, 1)
        key_block = lax.dynamic_slice_in_dim(key_heads, key_start, window, 1)
        value_block = lax.dynamic_slice_in_dim(value_heads, key_start, window, 1)
        query_docs = lax.dynamic_slice_in_dim(doc_ids, query_start, SEQ_DEV, 1)
        key_docs = lax.dynamic_slice_in_dim(doc_ids, key_start, window, 1)
        query_pos = query_start + jnp.arange(SEQ_DEV, dtype=jnp.int32)
        key_pos = key_start + jnp.arange(window, dtype=jnp.int32)
        scores = jnp.einsum('bqgrd,bkgd->bgrqk', query_block.astype(jnp.float32), key_block.astype(jnp.float32), precision=lax.Precision.HIGHEST) * scale
        allowed = (key_pos[None, :] <= query_pos[:, None])[None] & (key_docs[:, None, :] == query_docs[:, :, None])
        allowed = allowed[:, None, None]
        top = lax.optimization_barrier(jnp.max(jnp.where(allowed, scores, lowest), axis=-1, keepdims=True))
        probs = jnp.where(allowed, jnp.exp(scores - top), 0.0)
        total = lax.optimization_barrier(jnp.sum(probs, axis=-1))
        weights = probs.astype(jnp.bfloat16)
        mixed = jnp.einsum('bgrqk,bkgd->bgrqd', weights.astype(jnp.float32), value_block.astype(jnp.float32), precision=lax.Precision.HIGHEST)
        result = mixed / total[..., None]
        return jnp.transpose(result, (0, 3, 1, 2, 4)).astype(jnp.bfloat16)
    blocks = lax.map(one_block, jnp.arange(SEQ // SEQ_DEV, dtype=jnp.int32))
    blocks = jnp.moveaxis(blocks, 0, 1)
    return blocks.reshape(BATCH, SEQ, QH * HD)

def reference(mixer_input, gate_input, state_in, state_out, step_sizes, decay_rates, skip_gain, norm_gain, out_weight, queries, keys, values, doc_ids):
    inputs = mixer_input.reshape(BATCH, SEQ, H, P_SIZE)
    writers = state_in.reshape(BATCH, SEQ, G, N)
    readers = state_out.reshape(BATCH, SEQ, G, N)
    initial = jnp.zeros((BATCH, H, P_SIZE, N), jnp.float32)
    initial_doc = jnp.full((BATCH,), -1, jnp.int32)
    scanned, _ = span_scan(inputs, step_sizes, decay_rates, writers, readers, doc_ids, SPAN, initial, initial_doc)
    mixed = scanned + skip_gain[:, None] * inputs.astype(jnp.float32)
    gated = mixed.reshape(BATCH, SEQ, H * P_SIZE) * jax.nn.silu(gate_input.astype(jnp.float32))
    normed = gate_norm(gated, norm_gain, G).reshape(BATCH * SEQ, H * P_SIZE)
    rows = HEAD_DEV * P_SIZE
    summed = jnp.zeros((BATCH * SEQ, D), jnp.float32)
    for index in range(H // HEAD_DEV):
        partial_value = jnp.dot(normed[:, index * rows:(index + 1) * rows], out_weight[index * rows:(index + 1) * rows], preferred_element_type=jnp.float32)
        summed = summed + lax.optimization_barrier(partial_value.astype(jnp.bfloat16)).astype(jnp.float32)
    mixer_out = summed.reshape(BATCH, SEQ, D).astype(jnp.bfloat16)
    attn_out = attention(queries, keys, values, doc_ids)
    return (mixer_out, attn_out)
```

```python
import functools

import jax
import jax.numpy as jnp
from jax import lax
from jax.experimental import pallas as pl
from jax.experimental.pallas import tpu as pltpu
from jax.sharding import PartitionSpec as P

P_SIZE = 64
N = 128
HD = 128
LANES = 128
VMEM_LIMIT = 48 * 1024 * 1024

epsilon = 1e-05
lowest = -1e30


def halves(value):
    high = value.astype(jnp.bfloat16)
    low = (value - high.astype(jnp.float32)).astype(jnp.bfloat16)
    return jnp.concatenate([high, low], axis=-1)


def spreader(heads, first_head, channels):
    row = lax.broadcasted_iota(jnp.int32, (2 * heads, channels), 0)
    column = lax.broadcasted_iota(jnp.int32, (2 * heads, channels), 1)
    return (lax.rem(row, heads) == first_head + column // P_SIZE).astype(jnp.bfloat16)


def prepare_kernel(steps_ref, rates_ref, docs_ref, up_ref, down_ref, small_ref):
    steps = steps_ref[0]
    length, heads = steps.shape
    rate = steps * rates_ref[...]
    first = rate.astype(jnp.bfloat16)
    rest = rate - first.astype(jnp.float32)
    second = rest.astype(jnp.bfloat16)
    third = (rest - second.astype(jnp.float32)).astype(jnp.bfloat16)
    row = lax.broadcasted_iota(jnp.int32, (length, length), 0)
    column = lax.broadcasted_iota(jnp.int32, (length, length), 1)
    lower = (column <= row).astype(jnp.bfloat16)
    cumulative = sum(
        jnp.dot(lower, term, preferred_element_type=jnp.float32) for term in (first, second, third)
    )
    up_ref[0] = halves(jnp.exp(cumulative) * steps)
    down = jnp.exp(-cumulative)
    down_ref[0] = halves(down)
    small_ref[0] = jnp.concatenate([docs_ref[0], down[length - 1 :, :]], axis=-1)


def write_kernel(x_ref, up_ref, down_ref, writers_ref, tail_ref, scaled_ref, state_ref):
    channels = x_ref.shape[2]
    heads = up_ref.shape[2] // 2
    spread = spreader(heads, pl.program_id(1) * (channels // P_SIZE), channels)
    length = x_ref.shape[1]
    factor = jnp.dot(up_ref[0], spread, preferred_element_type=jnp.float32)
    scaled = (factor * x_ref[0].astype(jnp.float32)).astype(jnp.bfloat16)
    scaled_ref[0] = scaled
    ending = jnp.dot(
        down_ref[0, length - 16 :, :], spread, preferred_element_type=jnp.float32
    )[15:, :]
    writers = writers_ref[0] * tail_ref[0]
    state = lax.dot_general(
        writers, scaled, (((0,), (0,)), ((), ())), preferred_element_type=jnp.float32
    )
    state_ref[0] = (state * ending).astype(jnp.bfloat16)


def read_kernel(reach, *refs):
    (x_ref, scaled_ref, gate_ref, writers_ref, readers_ref, down_ref, column_ref, row_ref) = refs[:8]
    skip_ref, gain_ref, living_ref, through_ref = refs[8:12]
    state_refs = refs[12 : 12 + reach]
    out_ref = refs[12 + reach]
    length, channels = x_ref.shape[1:]
    heads = down_ref.shape[2] // 2
    spread = spreader(heads, pl.program_id(1) * (channels // P_SIZE), channels)
    row = lax.broadcasted_iota(jnp.int32, (length, length), 0)
    column = lax.broadcasted_iota(jnp.int32, (length, length), 1)
    allowed = (column <= row) & (column_ref[0] == row_ref[0])
    readers = readers_ref[0]
    inner = lax.dot_general(
        readers, writers_ref[0], (((1,), (1,)), ((), ())), preferred_element_type=jnp.float32
    )
    inner = jnp.where(allowed, inner, 0.0).astype(jnp.bfloat16)
    coefficients = jnp.dot(through_ref[0], spread, preferred_element_type=jnp.float32)
    before = state_refs[0][0].astype(jnp.float32)
    for index in range(1, reach):
        before = before + coefficients[index : index + 1, :] * state_refs[index][0].astype(
            jnp.float32
        )
    total = jnp.dot(inner, scaled_ref[0], preferred_element_type=jnp.float32)
    total = total + jnp.dot(
        readers * living_ref[0], before.astype(jnp.bfloat16), preferred_element_type=jnp.float32
    )
    factor = jnp.dot(down_ref[0], spread, preferred_element_type=jnp.float32)
    mixed = total * factor + skip_ref[...] * x_ref[0].astype(jnp.float32)
    gate = gate_ref[0].astype(jnp.float32)
    gated = mixed * (gate / (1.0 + jnp.exp(-gate)))
    square = jnp.mean(gated * gated, axis=-1, keepdims=True)
    out_ref[0] = (gated * lax.rsqrt(square + epsilon) * gain_ref[...]).astype(jnp.bfloat16)


def attention_kernel(blocks, *refs):
    queries_ref, column_ref, row_ref = refs[:3]
    key_refs = refs[3 : 3 + blocks]
    value_refs = refs[3 + blocks : 3 + 2 * blocks]
    out_ref = refs[3 + 2 * blocks]
    length = queries_ref.shape[1]
    keys = jnp.concatenate([ref[0] for ref in key_refs], axis=0)
    values = jnp.concatenate([ref[0] for ref in value_refs], axis=0)
    span = keys.shape[0]
    row = lax.broadcasted_iota(jnp.int32, (length, span), 0)
    column = lax.broadcasted_iota(jnp.int32, (length, span), 1)
    allowed = (column - (span - length) <= row) & (column_ref[0] == row_ref[0])
    scale = HD ** (-0.5)
    for head in range(queries_ref.shape[2] // HD):
        scores = lax.dot_general(
            queries_ref[0, :, head * HD : (head + 1) * HD],
            keys,
            (((1,), (1,)), ((), ())),
            preferred_element_type=jnp.float32,
        )
        scores = jnp.where(allowed, scores * scale, lowest)
        top = jnp.max(scores, axis=-1, keepdims=True)
        probs = jnp.exp(scores - top)
        total = jnp.sum(probs, axis=-1, keepdims=True)
        mixed = jnp.dot(probs.astype(jnp.bfloat16), values, preferred_element_type=jnp.float32)
        out_ref[0, :, head * HD : (head + 1) * HD] = (mixed / total).astype(jnp.bfloat16)


def params():
    return pltpu.CompilerParams(vmem_limit_bytes=VMEM_LIMIT)


def arriving(value, axis, by):
    devices = lax.axis_size(axis)
    return lax.ppermute(value, axis, [(i, i + by) for i in range(devices - by)])


def shards(
    mixer_input,
    gate_input,
    state_in,
    state_out,
    step_sizes,
    decay_rates,
    skip_gain,
    norm_gain,
    out_weight,
    queries,
    keys,
    values,
    doc_ids,
):
    batches, length, channels = mixer_input.shape
    heads = step_sizes.shape[2]
    groups = state_in.shape[2] // N
    wide = channels // groups
    reach = lax.axis_size("ctx") // 8
    f32, bf16 = jnp.float32, jnp.bfloat16
    struct = jax.ShapeDtypeStruct

    weight = gathered_weight(out_weight)

    docs = (doc_ids + 1).astype(f32)
    batch_block = lambda *shape: pl.BlockSpec((1,) + shape, lambda b: (b, 0, 0))
    up, down, small = pl.pallas_call(
        prepare_kernel,
        grid=(batches,),
        in_specs=[
            batch_block(length, heads),
            pl.BlockSpec((1, heads), lambda b: (0, 0)),
            batch_block(1, length),
        ],
        out_specs=[
            batch_block(length, 2 * heads),
            batch_block(length, 2 * heads),
            batch_block(1, length + heads),
        ],
        out_shape=[
            struct((batches, length, 2 * heads), bf16),
            struct((batches, length, 2 * heads), bf16),
            struct((batches, 1, length + heads), f32),
        ],
        name="prepare",
    )(step_sizes, decay_rates[None, :], docs[:, None, :])

    smalls = [arriving(small, "ctx", by) for by in range(1, reach + 1)]
    kept_keys, kept_values = [keys], [values]
    for by in range(1, reach + 1):
        kept_keys.append(arriving(kept_keys[-1], "ctx", 1))
        kept_values.append(arriving(kept_values[-1], "ctx", 1))

    up, kept_keys[1:], kept_values[1:] = lax.optimization_barrier(
        (up, kept_keys[1:], kept_values[1:])
    )
    last_doc = docs[:, -1:]
    tail = (docs == last_doc).astype(bf16)[:, :, None]
    per_batch = lambda *shape: pl.BlockSpec((1,) + shape, lambda b, g: (b, 0, 0))
    per_group = lambda rows, columns: pl.BlockSpec((1, rows, columns), lambda b, g: (b, 0, g))
    state_block = pl.BlockSpec((1, N, wide), lambda b, g: (b, 0, g))
    scaled, state = pl.pallas_call(
        write_kernel,
        grid=(batches, groups),
        in_specs=[
            per_group(length, wide),
            per_batch(length, 2 * heads),
            per_batch(length, 2 * heads),
            per_group(length, N),
            per_batch(length, 1),
        ],
        out_specs=[per_group(length, wide), state_block],
        out_shape=[
            struct((batches, length, channels), bf16),
            struct((batches, N, channels), bf16),
        ],
        compiler_params=params(),
        name="write_states",
    )(mixer_input, up, down, state_in, tail)
    states = [state]
    for by in range(1, reach + 1):
        states.append(arriving(states[-1], "ctx", 1))
    states = states[1:]

    near_doc = smalls[0][:, 0, length - 1]
    living = (docs == near_doc[:, None]).astype(bf16)[:, :, None]
    through = jnp.ones((batches, heads), f32)
    rows = [through]
    for by in range(1, reach):
        near, far = smalls[by - 1][:, 0], smalls[by][:, 0]
        passes = (near[:, 0] == near[:, length - 1]) & (near[:, 0] == far[:, length - 1])
        through = through * near[:, length:] * passes.astype(f32)[:, None]
        rows.append(through)
    rows += [jnp.zeros_like(through)] * (-len(rows) % 8)
    through = halves(jnp.stack(rows, axis=1))

    key_docs = jnp.concatenate([s[:, 0, :length] for s in smalls[::-1]] + [docs], axis=1)
    query_column = docs[:, :, None]
    blocks = reach + 1
    kv_heads = keys.shape[2] // HD
    repeat_wide = queries.shape[2] // kv_heads
    attn_out = pl.pallas_call(
        functools.partial(attention_kernel, blocks),
        grid=(batches, kv_heads),
        in_specs=[
            per_group(length, repeat_wide),
            per_batch(length, 1),
            per_batch(1, blocks * length),
        ]
        + [per_group(length, HD)] * (2 * blocks),
        out_specs=per_group(length, repeat_wide),
        out_shape=struct(queries.shape, bf16),
        compiler_params=params(),
        cost_estimate=pl.CostEstimate(
            flops=4 * queries.size * blocks * length * 8,
            bytes_accessed=40 * queries.size,
            transcendentals=queries.size * blocks * length // HD,
        ),
        name="attend",
    )(queries, query_column, key_docs[:, None, :], *kept_keys[::-1], *kept_values[::-1])

    attn_out, states = lax.optimization_barrier((attn_out, states))
    normed = pl.pallas_call(
        functools.partial(read_kernel, reach),
        grid=(batches, groups),
        in_specs=[
            per_group(length, wide),
            per_group(length, wide),
            per_group(length, wide),
            per_group(length, N),
            per_group(length, N),
            per_batch(length, 2 * heads),
            per_batch(length, 1),
            per_batch(1, length),
            pl.BlockSpec((1, wide), lambda b, g: (0, g)),
            pl.BlockSpec((1, wide), lambda b, g: (0, g)),
            per_batch(length, 1),
            per_batch(through.shape[1], 2 * heads),
        ]
        + [state_block] * reach,
        out_specs=per_group(length, wide),
        out_shape=struct((batches, length, channels), bf16),
        compiler_params=params(),
        name="read_states",
    )(
        mixer_input,
        scaled,
        gate_input,
        state_in,
        state_out,
        down,
        query_column,
        docs[:, None, :],
        jnp.repeat(skip_gain, P_SIZE)[None, :],
        norm_gain[None, :],
        living,
        through,
        *states,
    )
    mixer_out = project(normed, weight)
    return (mixer_out, attn_out)


def gathered_weight(out_weight):
    return lax.all_gather(out_weight, "ctx", axis=1, tiled=True)


def project(normed, weight):
    if lax.axis_size("head") != 2:
        projected = jnp.einsum("btc,cd->btd", normed, weight, preferred_element_type=jnp.float32)
        return lax.psum_scatter(
            projected.astype(jnp.bfloat16), "head", scatter_dimension=2, tiled=True
        )
    half, quarter = weight.shape[1] // 2, weight.shape[1] // 4
    mine = lax.axis_index("head")

    def product(start):
        block = lax.dynamic_slice_in_dim(weight, start, quarter, 1)
        result = jnp.einsum("btc,cd->btd", normed, block, preferred_element_type=jnp.float32)
        return result.astype(jnp.bfloat16)

    got = []
    for part in range(2):
        sent = product((1 - mine) * half + part * quarter)
        got.append(lax.ppermute(sent, "head", [(0, 1), (1, 0)]))
    kept = [product(mine * half + part * quarter) for part in range(2)]
    total = [a.astype(jnp.float32) + b.astype(jnp.float32) for a, b in zip(kept, got)]
    return jnp.concatenate(total, axis=2).astype(jnp.bfloat16)


def solution(mesh):
    in_specs = (
        P(None, "ctx", "head"),
        P(None, "ctx", "head"),
        P(None, "ctx", "head"),
        P(None, "ctx", "head"),
        P(None, "ctx", "head"),
        P("head"),
        P("head"),
        P("head"),
        P("head", "ctx"),
        P(None, "ctx", "head"),
        P(None, "ctx", "head"),
        P(None, "ctx", "head"),
        P(None, "ctx"),
    )
    out_specs = (P(None, "ctx", "head"), P(None, "ctx", "head"))
    return jax.shard_map(shards, mesh=mesh, in_specs=in_specs, out_specs=out_specs, check_vma=False)
```
